512 devices in a mesh: wide: 64 (over y, x, core), narrow: 8 (over z).
Axes of the slice: x: 4, y: 8, z: 8, core: 2. Of those that a mesh axis runs over, the one named last changes fastest.
Arguments:
- momentum: bfloat16 [16384, 16384], P('wide', 'narrow'), may hold values from -16 to 16
- basis: bfloat16 [8, 2048, 256], P('narrow', 'wide'), may hold values from -0.046875 to 0.046875
Outputs:
- momentum_new: float32 [16384, 16384], P('wide', 'narrow')
- direction: bfloat16 [16384, 16384], P('wide', 'narrow')
- basis_new: bfloat16 [8, 2048, 256], P('narrow', 'wide')
The draws below stay inside these ranges and needn't reach their ends.
All inputs are finite; a program needn't handle non-finite values.
Results may differ from the reference program's by a relative error of at most 0.015.
Values may be sent and summed in bfloat16 or wider, within the bound.
A program may use at most 64 MiB of HBM per device.

```python
import math
import jax
import jax.numpy as jnp
from jax import lax

M_ROWS = 16384
N = 16384
R = 256
ITERS = 2
N_NARROW = 8


def raised(drawn, own_key, source, target, parts, factor):
    def block_of(axis_at):
        return (jnp.arange(drawn.shape[axis_at]) // (drawn.shape[axis_at] // parts)).reshape((-1,) + (1,) * (drawn.ndim - 1 - axis_at))

    first = jax.random.permutation(own_key, parts)[block_of(target)]
    far = (block_of(target) + parts // 2) % parts
    return jnp.where((block_of(source) == first) | (block_of(source) == far), factor * drawn, drawn)


def block_scale(stream_key, extent, split, smallest, largest):
    factor_of, own = 1.0, jax.random.fold_in(stream_key, 6)
    for dim, parts in split:
        draws = jnp.exp(jax.random.uniform(jax.random.fold_in(own, dim), (parts,), jnp.float32, smallest / len(split), largest / len(split)))
        factor_of = factor_of * jnp.repeat(draws, extent[dim] // parts).reshape([-1 if axis == dim else 1 for axis in range(len(extent))])
    return factor_of


def noise(own_key, extent, deviation, reach, cuts=(), kind=jnp.bfloat16):
    result = deviation * jax.random.normal(own_key, extent, jnp.float32)
    if cuts:
        result = result * block_scale(own_key, extent, cuts, -0.22, 0.18)
    return jnp.clip(result, -reach, reach).astype(kind)


def heavy_noise(key, dims, spread, bound, shards, heavy, dtype=jnp.bfloat16):
    result = spread * jax.random.normal(key, dims, jnp.float32)
    if shards:
        result = result * block_scale(key, dims, shards, -0.22, 0.18)
    return jnp.clip(raised(result, jax.random.fold_in(key, 3), *heavy), -bound, bound).astype(dtype)


def setup_inputs(seed: int = 0) -> dict:
    arg_keys = jax.random.split(jax.random.key(seed), 3)
    return {
        "momentum": heavy_noise(arg_keys[0], (M_ROWS, N), 1.0, 16.0, ((0, 64), (1, 8)), (0, 1, 64, 4.0)),
        "basis": noise(arg_keys[1], (N_NARROW, N // N_NARROW, R), N ** -0.5, 0.046875, ((0, 8), (1, 64))),
    }


def reference(momentum, basis):
    buffer = momentum
    q_matrix = basis.reshape(N, R)
    for iteration in range(ITERS):
        summed = jnp.dot(buffer.astype(jnp.float32), q_matrix.astype(jnp.float32), preferred_element_type=jnp.float32)
        gram_matrix = jnp.dot(summed.T, summed, precision=lax.Precision.HIGHEST)
        factor = jnp.linalg.cholesky(gram_matrix)
        left_basis = lax.linalg.triangular_solve(factor, summed, left_side=False, lower=True, transpose_a=True).astype(jnp.bfloat16)
        right_full = jnp.dot(buffer.T.astype(jnp.float32), left_basis.astype(jnp.float32), preferred_element_type=jnp.float32)
        col_norms = jnp.sqrt(lax.optimization_barrier(jnp.sum(right_full * right_full, axis=0)) + 1e-06)
        q_matrix = (right_full / col_norms).astype(jnp.bfloat16)
    right_low = right_full.astype(jnp.bfloat16)
    feedback = jnp.dot(left_basis.astype(jnp.float32), right_low.T.astype(jnp.float32), preferred_element_type=jnp.float32)
    momentum_new = buffer.astype(jnp.float32) - 0.05 * feedback
    scaling = 0.25 * math.sqrt(M_ROWS * N / R)
    direction = (scaling * jnp.dot(left_basis.astype(jnp.float32), q_matrix.T.astype(jnp.float32), preferred_element_type=jnp.float32)).astype(jnp.bfloat16)
    return (momentum_new, direction, q_matrix.reshape(N_NARROW, N // N_NARROW, R))
```

```python
import functools
import math

import jax
import jax.numpy as jnp
from jax import lax
from jax.experimental import pallas as pl
from jax.experimental.pallas import tpu as pltpu
from jax.sharding import PartitionSpec as P

M_ROWS = 16384
N = 16384
R = 256
ITERS = 2
NC = 2
NX = 4
LEAF = 64
GROUP = 16
QUAD = 4
F32 = jnp.float32
BF16 = jnp.bfloat16
HIGHEST = lax.Precision.HIGHEST


def far_first(count):
    return sorted(range(1, count), key=lambda d: -min(d, count - d))


def dot_t(a, b):
    return lax.dot_general(a, b, (((1,), (1,)), ((), ())), preferred_element_type=F32, precision=HIGHEST)


def leaf_inverse(block):
    rows = lax.broadcasted_iota(jnp.int32, (LEAF, 2 * LEAF), 0)
    lanes = lax.broadcasted_iota(jnp.int32, (LEAF, 2 * LEAF), 1)
    eye = jnp.where(lanes == rows + LEAF, 1.0, 0.0).astype(F32)
    work = jnp.where(lanes < LEAF, jnp.concatenate([block, block], axis=1), eye)

    def group(step, work):
        alive = rows < LEAF - GROUP * step
        for first in range(0, GROUP, QUAD):
            cols = [jnp.broadcast_to(work[:, first + k : first + k + 1], (LEAF, 2 * LEAF)) for k in range(QUAD)]
            pivot_rows = [work[first + k : first + k + 1, :] for k in range(QUAD)]
            update = None
            for k in range(QUAD):
                at = first + k
                inverse = 1.0 / cols[k][at : at + 1, :]
                scaled = pivot_rows[k] * inverse
                for later in range(k + 1, QUAD):
                    ratio = cols[k][first + later : first + later + 1, :] * inverse
                    cols[later] = cols[later] - cols[k] * ratio
                    pivot_rows[later] = pivot_rows[later] - ratio * pivot_rows[k]
                term = jnp.where(alive & (rows > at), cols[k], 0.0) * scaled
                update = term if update is None else update + term
            work = work - update
        work = jnp.concatenate([work[GROUP:], work[:GROUP]], axis=0)
        return pltpu.roll(work, 2 * LEAF - GROUP, 1)

    work = lax.fori_loop(0, LEAF // GROUP, group, work)
    diagonal = jnp.sum(jnp.where(lanes == rows + LEAF, work, 0.0), axis=1, keepdims=True)
    return work[:, :LEAF] * (1.0 / jnp.sqrt(diagonal))


def inverse_factor(gram, work, inverse):
    work[...] = gram
    rows = lax.broadcasted_iota(jnp.int32, (R, R), 0)
    lanes = lax.broadcasted_iota(jnp.int32, (R, R), 1)
    inverse[...] = jnp.where(rows == lanes, 1.0, 0.0).astype(F32)
    for start in range(0, R, LEAF):
        stop = start + LEAF
        leaf = leaf_inverse(work[start:stop, start:stop])
        own = jnp.dot(leaf, inverse[start:stop, :], preferred_element_type=F32, precision=HIGHEST)
        inverse[start:stop, :] = own
        if stop < R:
            panel = jnp.dot(leaf, work[start:stop, :], preferred_element_type=F32, precision=HIGHEST)
            below = jnp.transpose(panel)[stop:, :]
            work[stop:, :] = work[stop:, :] - jnp.dot(below, panel, preferred_element_type=F32, precision=HIGHEST)
            inverse[stop:, :] = inverse[stop:, :] - jnp.dot(below, own, preferred_element_type=F32, precision=HIGHEST)


def kernel(sizes, m_ref, q_ref, left_out, right_out, norms_out, rows_out, mt, gathered, partial, partial_low, core_in, core_sum, x_in,
           x_low, y_in, z_out, z_in, z_all, square_all, g_out, g_core, g_sum, g_x, g_y_out, g_y_in, g_all, work, inverse, send, recv):
    ny, nz, block, tall = sizes
    w = lax.axis_index("wide")
    z = lax.axis_index("narrow")
    c, x, y = w % NC, (w // NC) % NX, w // (NC * NX)
    strip = tall // nz

    def core_peer():
        return {"wide": (y * NX + x) * NC + (1 - c)}

    def x_peer(d):
        return (x + d) % NX, {"wide": (y * NX + (x + d) % NX) * NC + c}

    def y_peer(d):
        return (y + d) % ny, {"wide": (((y + d) % ny) * NX + x) * NC + c}

    def z_peer(d):
        return (z + d) % nz, {"narrow": (z + d) % nz}

    barrier = pltpu.get_barrier_semaphore()
    peers = [core_peer()] + [x_peer(d)[1] for d in range(1, NX)] + [y_peer(d)[1] for d in range(1, ny)]
    peers += [z_peer(d)[1] for d in range(1, nz)]
    for peer in peers:
        pl.semaphore_signal(barrier, inc=1, device_id=peer, device_id_type=pl.DeviceIdType.MESH)
    pl.semaphore_wait(barrier, len(peers))

    sent = []

    def push(src, dst, peer):
        at = len(sent)
        copy = pltpu.make_async_remote_copy(src_ref=src, dst_ref=dst, send_sem=send.at[at], recv_sem=recv.at[at], device_id=peer,
                                            device_id_type=pl.DeviceIdType.MESH)
        copy.start()
        sent.append(copy)
        return copy

    def gather_plane(buf, beside=None):
        first = {d: push(buf.at[y, x, c], buf.at[y, x, c], y_peer(d)[1]) for d in far_first(ny)}
        if beside is not None:
            beside()
        for d in first:
            first[d].wait_recv()
        second = {d: push(buf.at[:, x, c], buf.at[:, x, c], x_peer(d)[1]) for d in far_first(NX)}
        third = [push(buf.at[:, x, c], buf.at[:, x, c], core_peer())]
        for d in sorted(second, key=lambda d: min(d, NX - d)):
            second[d].wait_recv()
            came = (x + NX - d) % NX
            third.append(push(buf.at[:, came, c], buf.at[:, came, c], core_peer()))
        for copy in third:
            copy.wait_recv()

    def exchange_narrow(buf):
        copies = [push(buf.at[z], buf.at[z], z_peer(d)[1]) for d in far_first(nz)]
        for copy in copies:
            copy.wait_recv()

    def transpose_momentum():
        def one(k, carry):
            at = pl.multiple_of(k * 256, 256)
            mt[pl.ds(at, 256), :] = jnp.transpose(m_ref[:, pl.ds(at, 256)])
            return carry

        lax.fori_loop(0, mt.shape[0] // 256, one, 0)

    def product(t):
        def one(k, total):
            at = pl.multiple_of(k * NX * NC * block, 256)
            q_part = gathered[t, k].reshape(NX * NC * block, R)
            return total + jnp.dot(m_ref[:, pl.ds(at, NX * NC * block)], q_part, preferred_element_type=F32)

        return lax.fori_loop(0, ny, one, jnp.zeros((tall, R), F32))

    def squares(t):
        def one(k, total):
            part = gathered[t, k].astype(F32).reshape(NX * NC * block, R)
            return total + jnp.sum((part * part).reshape(-1, 8, R), axis=0)

        total = lax.fori_loop(0, ny, one, jnp.zeros((8, R), F32))
        square_all[t, z] = total

    def norms(t):
        total = jnp.sum(square_all[t].reshape(nz * 8, R), axis=0, keepdims=True)
        return jnp.sqrt(total + 1e-06)

    def reduce_narrow(t, scale):
        copies = [push(z_out.at[t, z_peer(d)[0]], z_in.at[t, d - 1], z_peer(d)[1]) for d in far_first(nz)]
        total = z_out[t, z]
        for copy in copies:
            copy.wait_recv()
        for d in range(1, nz):
            total = total + z_in[t, d - 1]
        z_all[t, z] = total * scale() if scale is not None else total
        exchange_narrow(z_all.at[t])

    def reduce_gram(t):
        other = pl.ds(pl.multiple_of((1 - c) * (R // NC), 8), R // NC)
        mine = pl.ds(pl.multiple_of(c * (R // NC), 8), R // NC)
        push(g_out.at[t, other], g_core.at[t], core_peer()).wait_recv()
        g_sum[t] = (g_out[t, mine, :] + g_core[t]).reshape(NX, R // NC // NX, R)
        copies = [push(g_sum.at[t, x_peer(d)[0]], g_x.at[t, d - 1], x_peer(d)[1]) for d in far_first(NX)]
        total = g_sum[t, x]
        for copy in copies:
            copy.wait_recv()
        for d in range(1, NX):
            total = total + g_x[t, d - 1]
        total = total.reshape(ny // 2, -1, R)
        g_y_out[t, :, 0] = total[:, :, : R // 2]
        g_y_out[t, :, 1] = total[:, :, R // 2 :]
        copies = []
        for d in far_first(ny):
            to, peer = y_peer(d)
            copies.append(push(g_y_out.at[t, to // 2, to % 2], g_y_in.at[t, d - 1], peer))
        total = g_y_out[t, y // 2, y % 2]
        for copy in copies:
            copy.wait_recv()
        for d in range(1, ny):
            total = total + g_y_in[t, d - 1]
        mine = g_all.at[t, c, x, y // 2, y % 2]
        mine[...] = total
        copies = [push(mine, mine, y_peer(d)[1]) for d in far_first(ny)]
        for copy in copies:
            copy.wait_recv()
        mine = g_all.at[t, c, x]
        copies = [push(mine, mine, x_peer(d)[1]) for d in far_first(NX)]
        for copy in copies:
            copy.wait_recv()
        mine = g_all.at[t, c]
        push(mine, mine, core_peer()).wait_recv()
        halves = [g_all[t, :, :, :, h].reshape(R, R // 2) for h in range(2)]
        return jnp.concatenate(halves, axis=1)

    def back_product(t, left):
        def one(k, carry):
            at = pl.multiple_of(k * NX * NC * block, 256)
            part = jnp.dot(mt[pl.ds(at, NX * NC * block), :], left, preferred_element_type=F32)
            part = part.reshape(NX, NC, block, R)
            partial[t, k] = part
            partial_low[t, k] = part.astype(BF16)
            return carry

        lax.fori_loop(0, ny, one, 0)
        order = far_first(NX) + [0]
        first = {}
        for d in order:
            to = (x + d) % NX
            first[d] = push(partial_low.at[t, :, to, 1 - c], core_in.at[t, to], core_peer())
        second = []
        for d in order:
            to = (x + d) % NX
            first[d].wait_recv()
            total = partial[t, :, to, c] + core_in[t, to].astype(F32)
            if d:
                core_sum[t, d - 1] = total.astype(BF16)
                second.append(push(core_sum.at[t, d - 1], x_in.at[t, d - 1], x_peer(d)[1]))
        for copy in second:
            copy.wait_recv()
        for d in range(1, NX):
            total = total + x_in[t, d - 1].astype(F32)
        x_low[t] = total.astype(BF16)
        partial[t, :, x, c] = total
        third = [push(x_low.at[t, y_peer(d)[0]], y_in.at[t, d - 1], y_peer(d)[1]) for d in far_first(ny)]
        total = partial[t, y, x, c]
        for copy in third:
            copy.wait_recv()
        for d in range(1, ny):
            total = total + y_in[t, d - 1].astype(F32)
        return total

    gathered[0, y, x, c] = q_ref[...]
    gather_plane(gathered.at[0], transpose_momentum)
    for t in range(ITERS):
        z_out[t] = product(t).reshape(nz, strip, R)
        if t:
            squares(t)
            copies = [push(square_all.at[t, z], square_all.at[t, z], z_peer(d)[1]) for d in far_first(nz)]

            def scale():
                for copy in copies:
                    copy.wait_recv()
                return 1.0 / norms(t)

            reduce_narrow(t, scale)
        else:
            reduce_narrow(t, None)
        summed = z_all[t].reshape(tall, R)
        g_out[t] = jnp.dot(jnp.transpose(summed), summed, preferred_element_type=F32, precision=HIGHEST)
        inverse_factor(reduce_gram(t), work, inverse)
        left = dot_t(z_all[t].reshape(tall, R), inverse[...]).astype(BF16)
        right = back_product(t, left)
        gathered[t + 1, y, x, c] = right.astype(BF16)
        gather_plane(gathered.at[t + 1])
    squares(ITERS)
    exchange_narrow(square_all.at[ITERS])
    last = norms(ITERS)
    norms_out[...] = jnp.broadcast_to(last, (8, R))
    rows_out[...] = (right / last).astype(BF16)
    left_out[...] = left

    def give(k, carry):
        right_out[k] = gathered[ITERS, k].reshape(NX * NC * block, R)
        return carry

    lax.fori_loop(0, ny, give, 0)
    for copy in sent:
        copy.wait_send()


def count_copies(ny, nz):
    xs, ys, zs = NX - 1, ny - 1, nz - 1
    gather = ys + xs + NX
    one = zs + zs + 2 * (1 + xs + ys) + NX + xs + ys
    return (ITERS + 1) * gather + ITERS * one + ITERS * zs


def iterate(mesh, momentum, q_rows):
    ny, nz = mesh.shape["wide"] // (NC * NX), mesh.shape["narrow"]
    tall, broad = momentum.shape
    block = q_rows.shape[0]
    copies = count_copies(ny, nz)
    strip = tall // nz
    g_rows = R // (NC * NX * (ny // 2))
    vmem = pltpu.VMEM
    scratch = [
        vmem((broad, tall), BF16),
        vmem((ITERS + 1, ny, NX, NC, block, R), BF16),
        vmem((ITERS, ny, NX, NC, block, R), F32),
        vmem((ITERS, ny, NX, NC, block, R), BF16),
        vmem((ITERS, NX, ny, block, R), BF16),
        vmem((ITERS, NX - 1, ny, block, R), BF16),
        vmem((ITERS, NX - 1, ny, block, R), BF16),
        vmem((ITERS, ny, block, R), BF16),
        vmem((ITERS, ny - 1, block, R), BF16),
        vmem((ITERS, nz, strip, R), F32),
        vmem((ITERS, nz - 1, strip, R), F32),
        vmem((ITERS, nz, strip, R), F32),
        vmem((ITERS + 1, nz, 8, R), F32),
        vmem((ITERS, R, R), F32),
        vmem((ITERS, R // NC, R), F32),
        vmem((ITERS, NX, R // NC // NX, R), F32),
        vmem((ITERS, NX - 1, R // NC // NX, R), F32),
        vmem((ITERS, ny // 2, 2, g_rows, R // 2), F32),
        vmem((ITERS, ny - 1, g_rows, R // 2), F32),
        vmem((ITERS, NC, NX, ny // 2, 2, g_rows, R // 2), F32),
        vmem((R, R), F32),
        vmem((R, R), F32),
        pltpu.SemaphoreType.DMA((copies,)),
        pltpu.SemaphoreType.DMA((copies,)),
    ]
    whole = pl.BlockSpec(memory_space=pltpu.VMEM)
    return pl.pallas_call(
        functools.partial(kernel, (ny, nz, block, tall)),
        out_shape=(
            jax.ShapeDtypeStruct((tall, R), BF16),
            jax.ShapeDtypeStruct((ny, broad // ny, R), BF16),
            jax.ShapeDtypeStruct((8, R), F32),
            jax.ShapeDtypeStruct((block, R), BF16),
        ),
        in_specs=[whole] * 2,
        out_specs=(whole,) * 4,
        scratch_shapes=scratch,
        compiler_params=pltpu.CompilerParams(collective_id=0, has_side_effects=True, vmem_limit_bytes=48 * 1024 * 1024),
        name="iterate",
    )(momentum, q_rows)


def finish_kernel(scaling, m_ref, left_ref, right_ref, norms_ref, new_ref, direction_ref):
    left = left_ref[...]
    right = right_ref[...]
    outer = (((1,), (1,)), ((), ()))
    feedback = lax.dot_general(left, right, outer, preferred_element_type=F32)
    new_ref[...] = m_ref[...].astype(F32) - 0.05 * feedback
    q_block = (right.astype(F32) / norms_ref[0:1, :]).astype(BF16)
    product = lax.dot_general(left, q_block, outer, preferred_element_type=F32)
    direction_ref[...] = (scaling * product).astype(BF16)


def finish(momentum, left, right, norms):
    tall, broad = momentum.shape
    wide = 512 if broad % 512 == 0 else 256
    scaling = 0.25 * math.sqrt(M_ROWS * N / R)
    return pl.pallas_call(
        functools.partial(finish_kernel, scaling),
        grid=(broad // wide,),
        out_shape=(jax.ShapeDtypeStruct((tall, broad), F32), jax.ShapeDtypeStruct((tall, broad), BF16)),
        in_specs=[
            pl.BlockSpec((tall, wide), lambda j: (0, j)),
            pl.BlockSpec((tall, R), lambda j: (0, 0)),
            pl.BlockSpec((wide, R), lambda j: (j, 0)),
            pl.BlockSpec((8, R), lambda j: (0, 0)),
        ],
        out_specs=(pl.BlockSpec((tall, wide), lambda j: (0, j)), pl.BlockSpec((tall, wide), lambda j: (0, j))),
        name="finish",
    )(momentum, left, right, norms)


def on_device(mesh, momentum, basis):
    q_rows = basis.reshape(basis.shape[1], basis.shape[2])
    left, right, norms, rows = iterate(mesh, momentum, q_rows)
    momentum_new, direction = finish(momentum, left, right.reshape(-1, R), norms)
    return momentum_new, direction, rows.reshape(basis.shape)


def solution(mesh):
    placed = (P("wide", "narrow"), P("narrow", "wide", None))
    return jax.shard_map(
        functools.partial(on_device, mesh),
        mesh=mesh,
        in_specs=placed,
        out_specs=(P("wide", "narrow"), P("wide", "narrow"), P("narrow", "wide", None)),
        check_vma=False,
    )
```

```python
import functools
import math

import jax
import jax.numpy as jnp
from jax import lax
from jax.experimental import pallas as pl
from jax.experimental.pallas import tpu as pltpu
from jax.sharding import PartitionSpec as P

M_ROWS = 16384
N = 16384
R = 256
ITERS = 2
NC = 2
NX = 4
LEAF = 64
GROUP = 16
QUAD = 4
F32 = jnp.float32
BF16 = jnp.bfloat16
HIGHEST = lax.Precision.HIGHEST


def far_first(count):
    return sorted(range(1, count), key=lambda d: -min(d, count - d))


def dot_t(a, b):
    return lax.dot_general(a, b, (((1,), (1,)), ((), ())), preferred_element_type=F32, precision=HIGHEST)


def leaf_inverse(block):
    rows = lax.broadcasted_iota(jnp.int32, (LEAF, 2 * LEAF), 0)
    lanes = lax.broadcasted_iota(jnp.int32, (LEAF, 2 * LEAF), 1)
    eye = jnp.where(lanes == rows + LEAF, 1.0, 0.0).astype(F32)
    work = jnp.where(lanes < LEAF, jnp.concatenate([block, block], axis=1), eye)

    def group(step, work):
        alive = rows < LEAF - GROUP * step
        for first in range(0, GROUP, QUAD):
            cols = [jnp.broadcast_to(work[:, first + k : first + k + 1], (LEAF, 2 * LEAF)) for k in range(QUAD)]
            pivot_rows = [work[first + k : first + k + 1, :] for k in range(QUAD)]
            update = None
            for k in range(QUAD):
                at = first + k
                inverse = 1.0 / cols[k][at : at + 1, :]
                scaled = pivot_rows[k] * inverse
                for later in range(k + 1, QUAD):
                    ratio = cols[k][first + later : first + later + 1, :] * inverse
                    cols[later] = cols[later] - cols[k] * ratio
                    pivot_rows[later] = pivot_rows[later] - ratio * pivot_rows[k]
                term = jnp.where(alive & (rows > at), cols[k], 0.0) * scaled
                update = term if update is None else update + term
            work = work - update
        work = jnp.concatenate([work[GROUP:], work[:GROUP]], axis=0)
        return pltpu.roll(work, 2 * LEAF - GROUP, 1)

    work = lax.fori_loop(0, LEAF // GROUP, group, work)
    diagonal = jnp.sum(jnp.where(lanes == rows + LEAF, work, 0.0), axis=1, keepdims=True)
    return work[:, :LEAF] * (1.0 / jnp.sqrt(diagonal))


def inverse_factor(gram, work, inverse):
    work[...] = gram
    rows = lax.broadcasted_iota(jnp.int32, (R, R), 0)
    lanes = lax.broadcasted_iota(jnp.int32, (R, R), 1)
    inverse[...] = jnp.where(rows == lanes, 1.0, 0.0).astype(F32)
    for start in range(0, R, LEAF):
        stop = start + LEAF
        leaf = leaf_inverse(work[start:stop, start:stop])
        own = jnp.dot(leaf, inverse[start:stop, :], preferred_element_type=F32, precision=HIGHEST)
        inverse[start:stop, :] = own
        if stop < R:
            panel = jnp.dot(leaf, work[start:stop, :], preferred_element_type=F32, precision=HIGHEST)
            below = jnp.transpose(panel)[stop:, :]
            work[stop:, :] = work[stop:, :] - jnp.dot(below, panel, preferred_element_type=F32, precision=HIGHEST)
            inverse[stop:, :] = inverse[stop:, :] - jnp.dot(below, own, preferred_element_type=F32, precision=HIGHEST)


def kernel(sizes, m_hbm, q_hbm, left_out, right_out, norms_out, rows_out, m_ref, mt, gathered, partial, partial_low, core_in,
           core_sum, x_far, x_in, x_low, y_in, z_out, z_in, z_all, square_all, g_out, g_core, g_sum, g_x, g_y_out, g_y_in, g_z, g_all,
           work, inverse, send, recv, local):
    ny, nz, block, tall = sizes
    w = lax.axis_index("wide")
    z = lax.axis_index("narrow")
    c, x, y = w % NC, (w // NC) % NX, w // (NC * NX)
    strip = tall // nz
    half = ny // 2
    x_left, x_right, x_far_side = (x + NX - 1) % NX, (x + 1) % NX, (x + 2) % NX

    def core_peer():
        return {"wide": (y * NX + x) * NC + (1 - c)}

    def x_peer(d):
        return (x + d) % NX, {"wide": (y * NX + (x + d) % NX) * NC + c}

    def y_peer(d):
        return (y + d) % ny, {"wide": (((y + d) % ny) * NX + x) * NC + c}

    def z_peer(d):
        return (z + d) % nz, {"narrow": (z + d) % nz}

    load_m = pltpu.make_async_copy(m_hbm, m_ref, local.at[0])
    load_q = pltpu.make_async_copy(q_hbm, gathered.at[0, y, x, c], local.at[1])
    load_q.start()
    load_m.start()
    barrier = pltpu.get_barrier_semaphore()
    peers = [core_peer()] + [x_peer(d)[1] for d in range(1, NX)] + [y_peer(d)[1] for d in range(1, ny)]
    peers += [z_peer(d)[1] for d in range(1, nz)]
    for peer in peers:
        pl.semaphore_signal(barrier, inc=1, device_id=peer, device_id_type=pl.DeviceIdType.MESH)
    pl.semaphore_wait(barrier, len(peers))

    sent = []

    def push(src, dst, peer):
        at = len(sent)
        copy = pltpu.make_async_remote_copy(src_ref=src, dst_ref=dst, send_sem=send.at[at], recv_sem=recv.at[at], device_id=peer,
                                            device_id_type=pl.DeviceIdType.MESH)
        copy.start()
        sent.append(copy)
        return copy

    def gather_plane(buf, beside=None):
        own = buf.at[y, x, c]
        left, right = x_peer(NX - 1)[1], x_peer(1)[1]
        near = sorted(range(ny), key=lambda d: min(d, ny - d))
        from_y = {d: push(own, own, y_peer(d)[1]) for d in far_first(ny)}
        from_left, from_right, from_far = {}, {}, {}

        def spread(d):
            slot = buf.at[(y + ny - d) % ny, x, c]
            from_left[d] = push(slot, slot, right)
            from_right[d] = push(slot, slot, left)

        spread(0)
        if beside is not None:
            beside()
        for d in near[1:]:
            from_y[d].wait_recv()
            spread(d)
        across = [push(buf.at[:, x, c], buf.at[:, x, c], core_peer())]
        for d in near:
            row = (y + ny - d) % ny
            from_left[d].wait_recv()
            if d < half:
                from_far[d] = push(buf.at[row, x_left, c], buf.at[row, x_left, c], right)
            from_right[d].wait_recv()
            if d >= half:
                from_far[d] = push(buf.at[row, x_right, c], buf.at[row, x_right, c], left)
        for came in (x_left, x_right):
            across.append(push(buf.at[:, came, c], buf.at[:, came, c], core_peer()))
        for d in near:
            from_far[d].wait_recv()
        across.append(push(buf.at[:, x_far_side, c], buf.at[:, x_far_side, c], core_peer()))
        for copy in across:
            copy.wait_recv()

    def exchange_narrow(buf):
        copies = [push(buf.at[z], buf.at[z], z_peer(d)[1]) for d in far_first(nz)]
        for copy in copies:
            copy.wait_recv()

    def transpose_momentum():
        load_m.wait()

        def one(k, carry):
            at = pl.multiple_of(k * 256, 256)
            mt[pl.ds(at, 256), :] = jnp.transpose(m_ref[:, pl.ds(at, 256)])
            return carry

        lax.fori_loop(0, mt.shape[0] // 256, one, 0)

    def product(t):
        def one(k, total):
            at = pl.multiple_of(k * NX * NC * block, 256)
            q_part = gathered[t, k].reshape(NX * NC * block, R)
            return total + jnp.dot(m_ref[:, pl.ds(at, NX * NC * block)], q_part, preferred_element_type=F32)

        return lax.fori_loop(0, ny, one, jnp.zeros((tall, R), F32))

    def squares(t):
        def one(k, total):
            part = gathered[t, k].astype(F32).reshape(NX * NC * block, R)
            return total + jnp.sum((part * part).reshape(-1, 8, R), axis=0)

        total = lax.fori_loop(0, ny, one, jnp.zeros((8, R), F32))
        square_all[t, z] = total

    def norms(t):
        total = jnp.sum(square_all[t].reshape(nz * 8, R), axis=0, keepdims=True)
        return jnp.sqrt(total + 1e-06)

    def reduce_narrow(t, scale):
        copies = [push(z_out.at[t, z_peer(d)[0]], z_in.at[t, d - 1], z_peer(d)[1]) for d in far_first(nz)]
        total = z_out[t, z]
        for copy in copies:
            copy.wait_recv()
        for d in range(1, nz):
            total = total + z_in[t, d - 1]
        total = total * scale() if scale is not None else total
        z_all[t, z] = total
        return total

    def reduce_gram(t):
        other = pl.ds(pl.multiple_of((1 - c) * (R // NC), 8), R // NC)
        mine = pl.ds(pl.multiple_of(c * (R // NC), 8), R // NC)
        first = push(g_out.at[t, other], g_core.at[t], core_peer())
        strips = [push(z_all.at[t, z], z_all.at[t, z], z_peer(d)[1]) for d in far_first(nz)]
        first.wait_recv()
        g_sum[t] = (g_out[t, mine, :] + g_core[t]).reshape(NX, R // NC // NX, R)
        copies = [push(g_sum.at[t, x_peer(d)[0]], g_x.at[t, d - 1], x_peer(d)[1]) for d in far_first(NX)]
        total = g_sum[t, x]
        for copy in copies:
            copy.wait_recv()
        for d in range(1, NX):
            total = total + g_x[t, d - 1]
        total = total.reshape(ny // 2, -1, R)
        g_y_out[t, :, 0] = total[:, :, : R // 2]
        g_y_out[t, :, 1] = total[:, :, R // 2 :]
        copies = []
        for d in far_first(ny):
            to, peer = y_peer(d)
            copies.append(push(g_y_out.at[t, to // 2, to % 2], g_y_in.at[t, d - 1], peer))
        total = g_y_out[t, y // 2, y % 2]
        for copy in copies:
            copy.wait_recv()
        for d in range(1, ny):
            total = total + g_y_in[t, d - 1]
        g_z[t, z] = total
        exchange_narrow(g_z.at[t])
        total = g_z[t, 0]
        for k in range(1, nz):
            total = total + g_z[t, k]
        mine = g_all.at[t, c, x, y // 2, y % 2]
        mine[...] = total
        copies = [push(mine, mine, y_peer(d)[1]) for d in far_first(ny)]
        for copy in copies:
            copy.wait_recv()
        mine = g_all.at[t, c, x]
        copies = [push(mine, mine, x_peer(d)[1]) for d in far_first(NX)]
        for copy in copies:
            copy.wait_recv()
        mine = g_all.at[t, c]
        push(mine, mine, core_peer()).wait_recv()
        halves = [g_all[t, :, :, :, h].reshape(R, R // 2) for h in range(2)]
        return jnp.concatenate(halves, axis=1), strips

    def back_product(t, left_basis):
        left, right = x_peer(NX - 1)[1], x_peer(1)[1]
        low, high = pl.ds(0, half), pl.ds(half, half)
        from_core = {}
        for d in (2, 1, 3, 0):
            to = (x + d) % NX

            def one(k, carry):
                at = pl.multiple_of((k * NX + to) * (NC * block), NC * block)
                part = jnp.dot(mt[pl.ds(at, NC * block), :], left_basis, preferred_element_type=F32).reshape(NC, block, R)
                partial[t, k, to] = part
                partial_low[t, k, to] = part.astype(BF16)
                return carry

            lax.fori_loop(0, ny, one, 0)
            from_core[d] = push(partial_low.at[t, :, to, 1 - c], core_in.at[t, to], core_peer())

        def joined(d, rows):
            to = (x + d) % NX
            return partial[t, rows, to, c] + core_in[t, to, rows].astype(F32)

        def onward(d, rows, dst, peer, extra=None):
            total = joined(d, rows)
            if extra is not None:
                total = total + extra.astype(F32)
            core_sum[t, d - 1, rows] = total.astype(BF16)
            return push(core_sum.at[t, d - 1, rows], dst, peer)

        from_core[2].wait_recv()
        far_right = onward(2, low, x_far.at[t, 0], right)
        far_left = onward(2, high, x_far.at[t, 1], left)
        from_core[1].wait_recv()
        near = [onward(1, high, x_in.at[t, 0, high], right)]
        from_core[3].wait_recv()
        near.append(onward(3, low, x_in.at[t, 1, low], left))
        far_right.wait_recv()
        near.append(onward(1, low, x_in.at[t, 0, low], right, x_far[t, 0]))
        far_left.wait_recv()
        near.append(onward(3, high, x_in.at[t, 1, high], left, x_far[t, 1]))
        from_core[0].wait_recv()
        for copy in near:
            copy.wait_recv()
        total = joined(0, pl.ds(0, ny)) + x_in[t, 0].astype(F32) + x_in[t, 1].astype(F32)
        x_low[t] = total.astype(BF16)
        partial[t, :, x, c] = total
        third = [push(x_low.at[t, y_peer(d)[0]], y_in.at[t, d - 1], y_peer(d)[1]) for d in far_first(ny)]
        total = partial[t, y, x, c]
        for copy in third:
            copy.wait_recv()
        for d in range(1, ny):
            total = total + y_in[t, d - 1].astype(F32)
        return total

    load_q.wait()
    gather_plane(gathered.at[0], transpose_momentum)
    for t in range(ITERS):
        z_out[t] = product(t).reshape(nz, strip, R)
        if t:
            squares(t)
            copies = [push(square_all.at[t, z], square_all.at[t, z], z_peer(d)[1]) for d in far_first(nz)]

            def scale():
                for copy in copies:
                    copy.wait_recv()
                return 1.0 / norms(t)

            summed = reduce_narrow(t, scale)
        else:
            summed = reduce_narrow(t, None)
        g_out[t] = jnp.dot(jnp.transpose(summed), summed, preferred_element_type=F32, precision=HIGHEST)
        gram, strips = reduce_gram(t)
        inverse_factor(gram, work, inverse)
        for copy in strips:
            copy.wait_recv()
        left = dot_t(z_all[t].reshape(tall, R), inverse[...]).astype(BF16)
        right = back_product(t, left)
        gathered[t + 1, y, x, c] = right.astype(BF16)
        gather_plane(gathered.at[t + 1])
    squares(ITERS)
    exchange_narrow(square_all.at[ITERS])
    last = norms(ITERS)
    norms_out[...] = jnp.broadcast_to(last, (8, R))
    rows_out[...] = (right / last).astype(BF16)
    left_out[...] = left

    def give(k, carry):
        right_out[k] = gathered[ITERS, k].reshape(NX * NC * block, R)
        return carry

    lax.fori_loop(0, ny, give, 0)
    for copy in sent:
        copy.wait_send()


def count_copies(ny, nz):
    xs, ys, zs = NX - 1, ny - 1, nz - 1
    gather = ys + 3 * ny + NX
    one = 3 * zs + 2 * (1 + xs + ys) + NX + 6 + ys
    return (ITERS + 1) * gather + ITERS * one + ITERS * zs


def iterate(mesh, momentum, q_rows):
    ny, nz = mesh.shape["wide"] // (NC * NX), mesh.shape["narrow"]
    tall, broad = momentum.shape
    block = q_rows.shape[0]
    copies = count_copies(ny, nz)
    strip = tall // nz
    g_rows = R // (NC * NX * (ny // 2))
    vmem = pltpu.VMEM
    scratch = [
        vmem((tall, broad), BF16),
        vmem((broad, tall), BF16),
        vmem((ITERS + 1, ny, NX, NC, block, R), BF16),
        vmem((ITERS, ny, NX, NC, block, R), F32),
        vmem((ITERS, ny, NX, NC, block, R), BF16),
        vmem((ITERS, NX, ny, block, R), BF16),
        vmem((ITERS, NX - 1, ny, block, R), BF16),
        vmem((ITERS, 2, ny // 2, block, R), BF16),
        vmem((ITERS, 2, ny, block, R), BF16),
        vmem((ITERS, ny, block, R), BF16),
        vmem((ITERS, ny - 1, block, R), BF16),
        vmem((ITERS, nz, strip, R), F32),
        vmem((ITERS, nz - 1, strip, R), F32),
        vmem((ITERS, nz, strip, R), F32),
        vmem((ITERS + 1, nz, 8, R), F32),
        vmem((ITERS, R, R), F32),
        vmem((ITERS, R // NC, R), F32),
        vmem((ITERS, NX, R // NC // NX, R), F32),
        vmem((ITERS, NX - 1, R // NC // NX, R), F32),
        vmem((ITERS, ny // 2, 2, g_rows, R // 2), F32),
        vmem((ITERS, ny - 1, g_rows, R // 2), F32),
        vmem((ITERS, nz, g_rows, R // 2), F32),
        vmem((ITERS, NC, NX, ny // 2, 2, g_rows, R // 2), F32),
        vmem((R, R), F32),
        vmem((R, R), F32),
        pltpu.SemaphoreType.DMA((copies,)),
        pltpu.SemaphoreType.DMA((copies,)),
        pltpu.SemaphoreType.DMA((2,)),
    ]
    whole = pl.BlockSpec(memory_space=pltpu.VMEM)
    return pl.pallas_call(
        functools.partial(kernel, (ny, nz, block, tall)),
        out_shape=(
            jax.ShapeDtypeStruct((tall, R), BF16),
            jax.ShapeDtypeStruct((ny, broad // ny, R), BF16),
            jax.ShapeDtypeStruct((8, R), F32),
            jax.ShapeDtypeStruct((block, R), BF16),
        ),
        in_specs=[pl.BlockSpec(memory_space=pl.ANY)] * 2,
        out_specs=(whole,) * 4,
        scratch_shapes=scratch,
        compiler_params=pltpu.CompilerParams(collective_id=0, has_side_effects=True, vmem_limit_bytes=56 * 1024 * 1024),
        name="iterate",
    )(momentum, q_rows)


def finish_kernel(scaling, m_ref, left_ref, right_ref, norms_ref, new_ref, direction_ref):
    left = left_ref[...]
    right = right_ref[...]
    outer = (((1,), (1,)), ((), ()))
    feedback = lax.dot_general(left, right, outer, preferred_element_type=F32)
    new_ref[...] = m_ref[...].astype(F32) - 0.05 * feedback
    q_block = (right.astype(F32) / norms_ref[0:1, :]).astype(BF16)
    product = lax.dot_general(left, q_block, outer, preferred_element_type=F32)
    direction_ref[...] = (scaling * product).astype(BF16)


def finish(momentum, left, right, norms):
    tall, broad = momentum.shape
    wide = 512 if broad % 512 == 0 else 256
    scaling = 0.25 * math.sqrt(M_ROWS * N / R)
    return pl.pallas_call(
        functools.partial(finish_kernel, scaling),
        grid=(broad // wide,),
        out_shape=(jax.ShapeDtypeStruct((tall, broad), F32), jax.ShapeDtypeStruct((tall, broad), BF16)),
        in_specs=[
            pl.BlockSpec((tall, wide), lambda j: (0, j)),
            pl.BlockSpec((tall, R), lambda j: (0, 0)),
            pl.BlockSpec((wide, R), lambda j: (j, 0)),
            pl.BlockSpec((8, R), lambda j: (0, 0)),
        ],
        out_specs=(pl.BlockSpec((tall, wide), lambda j: (0, j)), pl.BlockSpec((tall, wide), lambda j: (0, j))),
        name="finish",
    )(momentum, left, right, norms)


def on_device(mesh, momentum, basis):
    q_rows = basis.reshape(basis.shape[1], basis.shape[2])
    left, right, norms, rows = iterate(mesh, momentum, q_rows)
    momentum_new, direction = finish(momentum, left, right.reshape(-1, R), norms)
    return momentum_new, direction, rows.reshape(basis.shape)


def solution(mesh):
    placed = (P("wide", "narrow"), P("narrow", "wide", None))
    return jax.shard_map(
        functools.partial(on_device, mesh),
        mesh=mesh,
        in_specs=placed,
        out_specs=(P("wide", "narrow"), P("wide", "narrow"), P("narrow", "wide", None)),
        check_vma=False,
    )
```
